512 devices in a mesh: grp: 2 (over core), row: 8 (over y), col: 32 (over x, z).
Axes of the slice: x: 4, y: 8, z: 8, core: 2. Of those that a mesh axis runs over, the one named last changes fastest.
Arguments:
- v_pppp: bfloat16 [2, 12288, 12288], P('grp', 'col', 'row'), may hold values from -0.0546875 to 0.0546875
- lam: bfloat16 [2, 1280, 12288], P('grp', 'row', 'col'), may hold values from -6 to 6
- v_hhpp: bfloat16 [2, 1280, 12288], P('grp', 'col', 'row'), may hold values from -6 to 6
- hole_energy: float32 [2, 1280], P('grp', 'col'), may hold values from -3 to -1
- part_energy: float32 [2, 12288], P('grp', 'row'), may hold values from 0.5 to 3
- pp_dim: int32 [2], P('grp'), may hold values from 3072 to 12288, as said below
- hh_dim: int32 [2], P('grp'), may hold values from 320 to 1280, as said below
Outputs:
- new_lam: bfloat16 [2, 1280, 12288], P('grp', 'col', 'row')
The draws below stay inside these ranges and needn't reach their ends.
Inputs may be any that keep to these rules, and one draw needn't show every extreme that they name: `pp_dim`: one channel, not always the same, uses all 12288 states; each uses at least a quarter of them. `hh_dim`: one channel, not always the same, uses all 1280 states; each uses at least a quarter of them.
All inputs are finite; a program needn't handle non-finite values.
Results may differ from the reference program's by a relative error of at most 0.019.
Values may be sent and summed in bfloat16 or wider, within the bound.
No kernel may reach another device: no remote copies, remote signals or barrier semaphores. Data moves between devices by JAX's collectives and lax.ppermute only.
A program may use at most 64 MiB of HBM per device.

```python
import jax
import jax.numpy as jnp
from jax import lax

P_SIZE = 12288
H = 1280
G = 2
N_COL = 32


def ragged_sizes(key, top):
    first, second = jax.random.split(key)
    others = jax.random.randint(first, (G,), top // 4, top + 1)
    full = jax.random.randint(second, (), 0, G)
    channel_ids = jnp.arange(G, dtype=jnp.int32)
    return jnp.where(channel_ids == full, top, others).astype(jnp.int32)


def draw_pp_dim(key, part):
    key = jax.random.fold_in(key, 11)
    return ragged_sizes(key, P_SIZE)


def draw_hh_dim(key, part):
    key = jax.random.fold_in(key, 23)
    return ragged_sizes(key, H)


def steps_of(rng, shape, cuts, least, high):
    def one(position, shards_of):
        draws = jax.random.uniform(jax.random.fold_in(jax.random.fold_in(rng, 6), position), (shards_of,), jnp.float32, least / len(cuts), high / len(cuts))
        return jnp.repeat(jnp.exp(draws), shape[position] // shards_of).reshape((-1,) + (1,) * (len(shape) - position - 1))

    gain = one(*cuts[0])
    for cut in cuts[1:]:
        gain = gain * one(*cut)
    return gain


def scatter_about(stream_key, dims, deviation, bound, cuts=(), kind=jnp.bfloat16):
    values = jax.random.normal(stream_key, dims, jnp.float32) * deviation
    if len(cuts) > 0:
        values = steps_of(stream_key, dims, cuts, -0.22, 0.18) * values
    return jnp.clip(values, min=-bound, max=bound).astype(kind)


def setup_inputs(seed: int = 0) -> dict:
    key_list = jax.random.split(jax.random.key(seed), 8)
    v_pppp = scatter_about(key_list[0], (G, P_SIZE, P_SIZE), P_SIZE ** -0.5, 0.0546875, ((0, 2), (1, 32), (2, 8)))
    lam = scatter_about(key_list[1], (G, H, P_SIZE), 1.0, 6.0, ((0, 2), (1, 8), (2, 32)))
    v_hhpp = scatter_about(key_list[2], (G, H, P_SIZE), 1.0, 6.0, ((0, 2), (1, 32), (2, 8)))
    hole_energy = jnp.clip(-3.0 + 2.0 * jax.random.uniform(key_list[3], (G, H), jnp.float32) ** steps_of(key_list[3], (G, H), ((0, 2), (1, 32)), -0.2, 0.2), -3.0, -1.0)
    part_energy = jnp.clip(0.5 + 2.5 * jax.random.uniform(key_list[4], (G, P_SIZE), jnp.float32) ** steps_of(key_list[4], (G, P_SIZE), ((0, 2), (1, 8)), -0.2, 0.2), 0.5, 3.0)
    pp_dim = draw_pp_dim(jax.random.fold_in(key_list[7], 71), 0)
    hh_dim = draw_hh_dim(jax.random.fold_in(key_list[7], 71), 0)
    return {"v_pppp": v_pppp, "lam": lam, "v_hhpp": v_hhpp, "hole_energy": hole_energy, "part_energy": part_energy, "pp_dim": pp_dim, "hh_dim": hh_dim}


def one_channel(vblock, lamg, vhh, hole, part, pdim, hdim):
    hh_ids = jnp.arange(H, dtype=jnp.int32)
    pp_ids = jnp.arange(P_SIZE, dtype=jnp.int32)
    keep = (hh_ids[:, None] < hdim) & (pp_ids[None, :] < pdim)
    masked = jnp.where(keep, lamg, jnp.zeros_like(lamg))
    width = P_SIZE // N_COL
    left_blocks = masked.reshape(H, N_COL, width).transpose(1, 0, 2)
    right_blocks = vblock.reshape(N_COL, width, P_SIZE)

    def add_block(total, pair):
        block_sum = jnp.dot(pair[0], pair[1], preferred_element_type=jnp.float32).astype(jnp.bfloat16)
        return total + block_sum.astype(jnp.float32), None

    ladder, unused = lax.scan(add_block, jnp.zeros((H, P_SIZE), jnp.float32), (left_blocks, right_blocks))
    denom = hole[:, None] - part[None, :]
    value = (vhh.astype(jnp.float32) + ladder) / denom
    return jnp.where(keep, value, jnp.zeros_like(value)).astype(jnp.bfloat16)


def reference(v_pppp, lam, v_hhpp, hole_energy, part_energy, pp_dim, hh_dim):
    outputs = []
    for index in range(G):
        outputs.append(one_channel(v_pppp[index], lam[index], v_hhpp[index], hole_energy[index], part_energy[index], pp_dim[index], hh_dim[index]))
    return jnp.stack(outputs)
```

```python
import jax
import jax.numpy as jnp
from jax import lax
from jax.sharding import PartitionSpec as P

NX, NZ, NY = 4, 8, 8


def ring_perm(axis, step):
    if axis == "y":
        return [(i, (i + step) % NY) for i in range(NY)]
    pairs = []
    for x in range(NX):
        for z in range(NZ):
            if axis == "x":
                pairs.append((x * NZ + z, ((x + step) % NX) * NZ + z))
            else:
                pairs.append((x * NZ + z, x * NZ + (z + step) % NZ))
    return pairs


def send(value, axis, step):
    return lax.ppermute(value, "row" if axis == "y" else "col", ring_perm(axis, step))


def gather_rows(shard, me):
    half = shard.shape[0] // 2
    out = jnp.zeros((NY,) + shard.shape, shard.dtype)
    put = lambda out, value, at, row: lax.dynamic_update_slice(out, value[None], (at % NY, row, 0))
    out = put(out, shard, me, 0)
    up = down = shard
    for s in range(1, NY // 2):
        up = send(up, "y", 1)
        down = send(down, "y", -1)
        out = put(out, up, me - s + NY, 0)
        out = put(out, down, me + s, 0)
    up = send(up[:half], "y", 1)
    down = send(down[half:], "y", -1)
    out = put(out, up, me + NY // 2, 0)
    out = put(out, down, me + NY // 2, half)
    return out


def ring_reduce(axis, size, me, part):
    far = size // 2
    up = send(part((me + far) % size, 0, 1).astype(jnp.bfloat16), axis, 1)
    down = send(part((me + far) % size, 1, 2).astype(jnp.bfloat16), axis, -1)
    for s in range(far - 1, 0, -1):
        mine_up = part((me + s) % size, 0, 2)
        mine_down = part((me - s + size) % size, 0, 2)
        if s == far - 1:
            up = jnp.concatenate([up, jnp.zeros_like(up)], axis=-1)
            down = jnp.concatenate([jnp.zeros_like(down), down], axis=-1)
        up = send((mine_up + up.astype(jnp.float32)).astype(jnp.bfloat16), axis, 1)
        down = send((mine_down + down.astype(jnp.float32)).astype(jnp.bfloat16), axis, -1)
    return part(me, 0, 2) + up.astype(jnp.float32) + down.astype(jnp.float32)


def local(v_pppp, lam, v_hhpp, hole_energy, part_energy, pp_dim, hh_dim):
    pp_used = pp_dim[0]
    hh_used = hh_dim[0]
    hole_local = lam.shape[1]
    part_local = lam.shape[2]
    y = lax.axis_index("row")
    col = lax.axis_index("col")
    x, z = col // NZ, col % NZ
    hole_ids = y * hole_local + jnp.arange(hole_local, dtype=jnp.int32)
    part_ids = col * part_local + jnp.arange(part_local, dtype=jnp.int32)
    keep = (hole_ids[:, None] < hh_used) & (part_ids[None, :] < pp_used)
    masked = jnp.where(keep, lam[0], jnp.zeros_like(lam[0]))
    out_rows = v_hhpp.shape[1]
    out_cols = v_hhpp.shape[2]
    left = gather_rows(masked, y).reshape(NX, NZ, out_rows, part_local)
    tile = v_pppp[0]
    mid = out_cols // 2
    dot = lambda a, b: jnp.dot(a, b, preferred_element_type=jnp.float32)

    def z_term(owner, lo, hi):
        rows = lax.dynamic_slice_in_dim(left, owner, 1, 1).reshape(NX * out_rows, part_local)
        return dot(rows, tile[:, lo * (mid // 2) : hi * (mid // 2)])

    def x_term(owner, lo, hi):
        rows = lax.dynamic_slice_in_dim(left, owner, 1, 0).reshape(NZ * out_rows, part_local)
        return dot(rows, tile[:, mid + lo * (mid // 2) : mid + hi * (mid // 2)])

    by_z = ring_reduce("z", NZ, z, z_term).reshape(NX, out_rows, mid)
    by_x = ring_reduce("x", NX, x, x_term).reshape(NZ, out_rows, mid)

    def rest_of(parts):
        def term(owner, lo, hi):
            block = lax.dynamic_slice_in_dim(parts, owner, 1, 0)[0]
            return block[:, lo * (mid // 2) : hi * (mid // 2)]

        return term

    first = ring_reduce("x", NX, x, rest_of(by_z))
    second = ring_reduce("z", NZ, z, rest_of(by_x))
    ladder = jnp.concatenate([first, second], axis=1)
    out_hole = col * out_rows + jnp.arange(out_rows, dtype=jnp.int32)
    out_part = y * out_cols + jnp.arange(out_cols, dtype=jnp.int32)
    valid = (out_hole[:, None] < hh_used) & (out_part[None, :] < pp_used)
    denom = hole_energy[0][:, None] - part_energy[0][None, :]
    value = (v_hhpp[0].astype(jnp.float32) + ladder) / denom
    result = jnp.where(valid, value, jnp.zeros_like(value)).astype(jnp.bfloat16)
    return result[None]


def solution(mesh):
    return jax.shard_map(
        local,
        mesh=mesh,
        in_specs=(
            P("grp", "col", "row"),
            P("grp", "row", "col"),
            P("grp", "col", "row"),
            P("grp", "col"),
            P("grp", "row"),
            P("grp"),
            P("grp"),
        ),
        out_specs=P("grp", "col", "row"),
        check_vma=False,
    )
```

```python
import jax
import jax.numpy as jnp
from jax import lax
from jax.sharding import Mesh, PartitionSpec as P

NX, NZ, NY = 4, 8, 8
COLS_A = 1024


def exchange_sum(parts, axis):
    got = lax.all_to_all(parts, axis, 0, 0)
    return jnp.sum(got.astype(jnp.float32), axis=0)


def local(v_pppp, lam, v_hhpp, hole_energy, part_energy, pp_dim, hh_dim):
    pp_used = pp_dim[0]
    hh_used = hh_dim[0]
    hole_local = lam.shape[1]
    part_local = lam.shape[2]
    y = lax.axis_index("row")
    col = lax.axis_index("x") * NZ + lax.axis_index("z")
    hole_ids = y * hole_local + jnp.arange(hole_local, dtype=jnp.int32)
    part_ids = col * part_local + jnp.arange(part_local, dtype=jnp.int32)
    keep = (hole_ids[:, None] < hh_used) & (part_ids[None, :] < pp_used)
    masked = jnp.where(keep, lam[0], jnp.zeros_like(lam[0]))
    out_rows = v_hhpp.shape[1]
    out_cols = v_hhpp.shape[2]
    left = lax.all_gather(masked, "row", axis=0, tiled=True)
    by_owner = left.reshape(NX, NZ, out_rows, part_local)
    left_z = by_owner.transpose(1, 0, 2, 3).reshape(NX * NZ * out_rows, part_local)
    tile = v_pppp[0]
    dot = lambda a, b: jnp.dot(a, b, preferred_element_type=jnp.float32).astype(jnp.bfloat16)

    part_a = dot(left_z, tile[:, :COLS_A])
    sum_a = lax.psum_scatter(part_a, "z", scatter_dimension=0, tiled=True)
    part_b = dot(left, tile[:, COLS_A:])
    cols_b = out_cols - COLS_A
    sum_b = exchange_sum(part_b.reshape(NX, NZ * out_rows, cols_b), "x").astype(jnp.bfloat16)
    ladder_b = exchange_sum(sum_b.reshape(NZ, out_rows, cols_b), "z")
    ladder_a = exchange_sum(sum_a.reshape(NX, out_rows, COLS_A), "x")
    ladder = jnp.concatenate([ladder_a, ladder_b], axis=1)

    out_hole = col * out_rows + jnp.arange(out_rows, dtype=jnp.int32)
    out_part = y * out_cols + jnp.arange(out_cols, dtype=jnp.int32)
    valid = (out_hole[:, None] < hh_used) & (out_part[None, :] < pp_used)
    denom = hole_energy[0][:, None] - part_energy[0][None, :]
    value = (v_hhpp[0].astype(jnp.float32) + ladder) / denom
    result = jnp.where(valid, value, jnp.zeros_like(value)).astype(jnp.bfloat16)
    return result[None]


def solution(mesh):
    split = Mesh(mesh.devices.reshape(2, NY, NX, NZ), ("grp", "row", "x", "z"))
    col = ("x", "z")
    return jax.shard_map(
        local,
        mesh=split,
        in_specs=(
            P("grp", col, "row"),
            P("grp", "row", col),
            P("grp", col, "row"),
            P("grp", col),
            P("grp", "row"),
            P("grp"),
            P("grp"),
        ),
        out_specs=P("grp", col, "row"),
        check_vma=False,
    )
```

```python
import jax
import jax.numpy as jnp
from jax import lax
from jax.sharding import Mesh, PartitionSpec as P

NX, NZ, NY = 4, 8, 8
PAIR = 2


def local(v_pppp, lam, v_hhpp, hole_energy, part_energy, pp_dim, hh_dim):
    pp_used = pp_dim[0]
    hh_used = hh_dim[0]
    hole_local = lam.shape[1]
    part_local = lam.shape[2]
    y = lax.axis_index("row")
    col = lax.axis_index(("x", "zh", "zl"))
    hole_ids = y * hole_local + jnp.arange(hole_local, dtype=jnp.int32)
    part_ids = col * part_local + jnp.arange(part_local, dtype=jnp.int32)
    keep = (hole_ids[:, None] < hh_used) & (part_ids[None, :] < pp_used)
    masked = jnp.where(keep, lam[0], jnp.zeros_like(lam[0]))
    out_rows = v_hhpp.shape[1]
    out_cols = v_hhpp.shape[2]
    left = lax.all_gather(masked, "row", axis=0, tiled=True)

    by_owner = left.reshape(NX, NZ // PAIR, PAIR, out_rows, part_local).transpose(0, 2, 1, 3, 4)
    part = jnp.dot(by_owner.reshape(NX * NZ * out_rows, part_local), v_pppp[0], preferred_element_type=jnp.float32)
    part = part.astype(jnp.bfloat16).reshape(NX * PAIR, NZ // PAIR * out_rows, out_cols)
    got = lax.all_to_all(part, ("x", "zl"), 0, 0)
    some = jnp.sum(got.astype(jnp.float32), axis=0).astype(jnp.bfloat16)
    got = lax.all_to_all(some.reshape(NZ // PAIR, out_rows, out_cols), "zh", 0, 0)
    ladder = jnp.sum(got.astype(jnp.float32), axis=0)

    out_hole = col * out_rows + jnp.arange(out_rows, dtype=jnp.int32)
    out_part = y * out_cols + jnp.arange(out_cols, dtype=jnp.int32)
    valid = (out_hole[:, None] < hh_used) & (out_part[None, :] < pp_used)
    denom = hole_energy[0][:, None] - part_energy[0][None, :]
    value = (v_hhpp[0].astype(jnp.float32) + ladder) / denom
    result = jnp.where(valid, value, jnp.zeros_like(value)).astype(jnp.bfloat16)
    return result[None]


def solution(mesh):
    split = Mesh(mesh.devices.reshape(2, NY, NX, NZ // PAIR, PAIR), ("grp", "row", "x", "zh", "zl"))
    col = ("x", "zh", "zl")
    return jax.shard_map(
        local,
        mesh=split,
        in_specs=(
            P("grp", col, "row"),
            P("grp", "row", col),
            P("grp", col, "row"),
            P("grp", col),
            P("grp", "row"),
            P("grp"),
            P("grp"),
        ),
        out_specs=P("grp", col, "row"),
        check_vma=False,
    )
```

```python
import jax
import jax.numpy as jnp
from jax import lax
from jax.sharding import Mesh, PartitionSpec as P

NX, NZ, NY = 4, 8, 8
PAIR = 2


def local(v_pppp, lam, v_hhpp, hole_energy, part_energy, pp_dim, hh_dim):
    pp_used = pp_dim[0]
    hh_used = hh_dim[0]
    hole_local = lam.shape[1]
    part_local = lam.shape[2]
    y = lax.axis_index("row")
    col = lax.axis_index(("x", "zh", "zl"))
    hole_ids = y * hole_local + jnp.arange(hole_local, dtype=jnp.int32)
    part_ids = col * part_local + jnp.arange(part_local, dtype=jnp.int32)
    keep = (hole_ids[:, None] < hh_used) & (part_ids[None, :] < pp_used)
    masked = jnp.where(keep, lam[0], jnp.zeros_like(lam[0]))
    out_rows = v_hhpp.shape[1]
    out_cols = v_hhpp.shape[2]
    swap = [(0, 1), (1, 0)]
    odd = lax.axis_index("zl") == 1

    halves = masked.reshape(hole_local // (PAIR * out_rows), PAIR, out_rows, part_local)
    half = (hole_local // PAIR, part_local)
    kept = jnp.where(odd, halves[:, 1], halves[:, 0]).reshape(half)
    given = jnp.where(odd, halves[:, 0], halves[:, 1]).reshape(half)
    taken = lax.ppermute(given, "zl", swap)
    tile, taken = lax.optimization_barrier((v_pppp[0], taken))
    other_tile = lax.ppermute(tile, "zl", swap)
    left = lax.all_gather(jnp.concatenate([kept, taken], axis=1), "row", axis=0, tiled=True)
    part = jnp.dot(left[:, :part_local], tile, preferred_element_type=jnp.float32)
    part = part + jnp.dot(left[:, part_local:], other_tile, preferred_element_type=jnp.float32)

    part = part.astype(jnp.bfloat16).reshape(NX, NZ // PAIR * out_rows, out_cols)
    got = lax.all_to_all(part, "x", 0, 0)
    some = jnp.sum(got.astype(jnp.float32), axis=0).astype(jnp.bfloat16)
    got = lax.all_to_all(some.reshape(NZ // PAIR, out_rows, out_cols), "zh", 0, 0)
    ladder = jnp.sum(got.astype(jnp.float32), axis=0)

    out_hole = col * out_rows + jnp.arange(out_rows, dtype=jnp.int32)
    out_part = y * out_cols + jnp.arange(out_cols, dtype=jnp.int32)
    valid = (out_hole[:, None] < hh_used) & (out_part[None, :] < pp_used)
    denom = hole_energy[0][:, None] - part_energy[0][None, :]
    value = (v_hhpp[0].astype(jnp.float32) + ladder) / denom
    result = jnp.where(valid, value, jnp.zeros_like(value)).astype(jnp.bfloat16)
    return result[None]


def solution(mesh):
    split = Mesh(mesh.devices.reshape(2, NY, NX, NZ // PAIR, PAIR), ("grp", "row", "x", "zh", "zl"))
    col = ("x", "zh", "zl")
    return jax.shard_map(
        local,
        mesh=split,
        in_specs=(
            P("grp", col, "row"),
            P("grp", "row", col),
            P("grp", col, "row"),
            P("grp", col),
            P("grp", "row"),
            P("grp"),
            P("grp"),
        ),
        out_specs=P("grp", col, "row"),
        check_vma=False,
    )
```

```python
import jax
import jax.numpy as jnp
from jax import lax
from jax.sharding import Mesh, PartitionSpec as P

NX, NZ, NY = 4, 8, 8
PAIR = 2


def add_up(parts):
    total = parts[0].astype(jnp.float32)
    for i in range(1, parts.shape[0]):
        total = total + parts[i].astype(jnp.float32)
    return total


def local(v_pppp, lam, v_hhpp, hole_energy, part_energy, pp_dim, hh_dim):
    pp_used = pp_dim[0]
    hh_used = hh_dim[0]
    hole_local = lam.shape[1]
    part_local = lam.shape[2]
    y = lax.axis_index("row")
    col = lax.axis_index(("x", "zh", "zl"))
    out_rows = v_hhpp.shape[1]
    out_cols = v_hhpp.shape[2]
    swap = [(0, 1), (1, 0)]
    odd = lax.axis_index("zl") == 1

    halves = lam[0].reshape(hole_local // (PAIR * out_rows), PAIR, out_rows, part_local)
    half = (hole_local // PAIR, part_local)
    kept = jnp.where(odd, halves[:, 1], halves[:, 0]).reshape(half)
    given = jnp.where(odd, halves[:, 0], halves[:, 1]).reshape(half)
    taken = lax.ppermute(given, "zl", swap)
    tile, taken = lax.optimization_barrier((v_pppp[0], taken))
    other_tile = lax.ppermute(tile, "zl", swap)
    place = lax.axis_index("zl")
    blocks = jnp.arange(hole_local // (PAIR * out_rows), dtype=jnp.int32)
    hole_ids = y * hole_local + (blocks[:, None] * PAIR + place) * out_rows + jnp.arange(out_rows, dtype=jnp.int32)
    part_ids = jnp.stack([col, col + 1 - 2 * place])[:, None] * part_local + jnp.arange(part_local, dtype=jnp.int32)
    keep = (hole_ids.reshape(-1, 1) < hh_used) & (part_ids.reshape(1, -1) < pp_used)
    both = jnp.concatenate([kept, taken], axis=1)
    both = jnp.where(keep, both, jnp.zeros_like(both))
    left = lax.all_gather(both, "row", axis=0, tiled=True)
    out_hole = col * out_rows + jnp.arange(out_rows, dtype=jnp.int32)
    out_part = y * out_cols + jnp.arange(out_cols, dtype=jnp.int32)
    ends = (out_hole < hh_used, out_part < pp_used, hole_energy[0], part_energy[0])
    left, ends = lax.optimization_barrier((left, ends))
    row_ok, col_ok, hole, particle = ends
    part = jnp.dot(left[:, :part_local], tile, preferred_element_type=jnp.float32)
    part = part + jnp.dot(left[:, part_local:], other_tile, preferred_element_type=jnp.float32)

    part = part.astype(jnp.bfloat16).reshape(NX, NZ // PAIR * out_rows, out_cols)
    got = lax.all_to_all(part, "x", 0, 0)
    some = add_up(got).astype(jnp.bfloat16)
    got = lax.all_to_all(some.reshape(NZ // PAIR, out_rows, out_cols), "zh", 0, 0)
    ladder = add_up(got)

    valid = row_ok[:, None] & col_ok[None, :]
    denom = hole[:, None] - particle[None, :]
    value = (v_hhpp[0].astype(jnp.float32) + ladder) / denom
    result = jnp.where(valid, value, jnp.zeros_like(value)).astype(jnp.bfloat16)
    return result[None]


def solution(mesh):
    split = Mesh(mesh.devices.reshape(2, NY, NX, NZ // PAIR, PAIR), ("grp", "row", "x", "zh", "zl"))
    col = ("x", "zh", "zl")
    return jax.shard_map(
        local,
        mesh=split,
        in_specs=(
            P("grp", col, "row"),
            P("grp", "row", col),
            P("grp", col, "row"),
            P("grp", col),
            P("grp", "row"),
            P("grp"),
            P("grp"),
        ),
        out_specs=P("grp", col, "row"),
        check_vma=False,
    )
```

```python
import jax
import jax.numpy as jnp
from jax import lax
from jax.sharding import Mesh, PartitionSpec as P

NX, NZ, NY = 4, 8, 8
PAIR = 2


def add_up(parts):
    total = parts[0].astype(jnp.float32)
    for i in range(1, parts.shape[0]):
        total = total + parts[i].astype(jnp.float32)
    return total


def local(v_pppp, lam, v_hhpp, hole_energy, part_energy, pp_dim, hh_dim):
    pp_used = pp_dim[0]
    hh_used = hh_dim[0]
    hole_local = lam.shape[1]
    part_local = lam.shape[2]
    y = lax.axis_index("row")
    col = lax.axis_index(("x", "zh", "zl"))
    out_rows = v_hhpp.shape[1]
    out_cols = v_hhpp.shape[2]
    swap = [(0, 1), (1, 0)]

    halves = lam[0].reshape(hole_local // (PAIR * out_rows), PAIR, out_rows, part_local)
    half = (hole_local // PAIR, part_local)
    place = lax.axis_index("zl")
    kept = lax.dynamic_slice_in_dim(halves, place, 1, 1).reshape(half)
    pair = lax.all_gather(halves, "zl")
    tile, pair = lax.optimization_barrier((v_pppp[0], pair))
    taken = lax.dynamic_slice(pair, (1 - place, 0, place, 0, 0), (1, hole_local // (PAIR * out_rows), 1, out_rows, part_local)).reshape(half)
    other_tile = lax.ppermute(tile, "zl", swap)
    blocks = jnp.arange(hole_local // (PAIR * out_rows), dtype=jnp.int32)
    hole_ids = y * hole_local + (blocks[:, None] * PAIR + place) * out_rows + jnp.arange(out_rows, dtype=jnp.int32)
    part_ids = jnp.stack([col, col + 1 - 2 * place])[:, None] * part_local + jnp.arange(part_local, dtype=jnp.int32)
    keep = (hole_ids.reshape(-1, 1) < hh_used) & (part_ids.reshape(1, -1) < pp_used)
    both = jnp.concatenate([kept, taken], axis=1)
    both = jnp.where(keep, both, jnp.zeros_like(both))
    left = lax.all_gather(both, "row", axis=0, tiled=True)
    out_hole = col * out_rows + jnp.arange(out_rows, dtype=jnp.int32)
    out_part = y * out_cols + jnp.arange(out_cols, dtype=jnp.int32)
    ends = (out_hole < hh_used, out_part < pp_used, hole_energy[0], part_energy)
    left, ends = lax.optimization_barrier((left, ends))
    row_ok, col_ok, hole, particle = ends
    part = jnp.dot(left[:, :part_local], tile, preferred_element_type=jnp.float32)
    part = part + jnp.dot(left[:, part_local:], other_tile, preferred_element_type=jnp.float32)

    part = part.astype(jnp.bfloat16).reshape(NX, NZ // PAIR * out_rows, out_cols)
    got = lax.all_to_all(part, "x", 0, 0)
    some = add_up(got).astype(jnp.bfloat16)
    got = lax.all_to_all(some.reshape(NZ // PAIR, out_rows, out_cols), "zh", 0, 0)
    ladder = add_up(got)

    valid = row_ok[:, None] & col_ok[None, :]
    denom = hole[:, None] - particle
    value = (v_hhpp[0].astype(jnp.float32) + ladder) / denom
    result = jnp.where(valid, value, jnp.zeros_like(value)).astype(jnp.bfloat16)
    return result[None]


def solution(mesh):
    split = Mesh(mesh.devices.reshape(2, NY, NX, NZ // PAIR, PAIR), ("grp", "row", "x", "zh", "zl"))
    col = ("x", "zh", "zl")
    return jax.shard_map(
        local,
        mesh=split,
        in_specs=(
            P("grp", col, "row"),
            P("grp", "row", col),
            P("grp", col, "row"),
            P("grp", col),
            P("grp", "row"),
            P("grp"),
            P("grp"),
        ),
        out_specs=P("grp", col, "row"),
        check_vma=False,
    )
```

```python
import jax
import jax.numpy as jnp
from jax import lax
from jax.sharding import Mesh, PartitionSpec as P

NX, NZ, NY = 4, 8, 8
PAIR = 2


def add_up(parts):
    total = parts[0].astype(jnp.float32)
    for i in range(1, parts.shape[0]):
        total = total + parts[i].astype(jnp.float32)
    return total


def local(v_pppp, lam, v_hhpp, hole_energy, part_energy, pp_dim, hh_dim):
    pp_used = pp_dim[0]
    hh_used = hh_dim[0]
    hole_local = lam.shape[1]
    part_local = lam.shape[2]
    y = lax.axis_index("row")
    col = lax.axis_index(("x", "zh", "zl"))
    out_rows = v_hhpp.shape[1]
    out_cols = v_hhpp.shape[2]
    swap = [(0, 1), (1, 0)]

    halves = lam[0].reshape(hole_local // (PAIR * out_rows), PAIR, out_rows, part_local)
    half = (hole_local // PAIR, part_local)
    place = lax.axis_index("zl")
    kept = lax.dynamic_slice_in_dim(halves, place, 1, 1).reshape(half)
    given = lax.dynamic_slice_in_dim(halves, 1 - place, 1, 1).reshape(half)
    kept, given = lax.optimization_barrier((kept, given))
    pair = lax.all_gather(given, "zl")
    tile, pair = lax.optimization_barrier((v_pppp[0], pair))
    taken = jnp.where(place == 1, pair[0], pair[1])
    other_tile = lax.ppermute(tile, "zl", swap)
    blocks = jnp.arange(hole_local // (PAIR * out_rows), dtype=jnp.int32)
    hole_ids = y * hole_local + (blocks[:, None] * PAIR + place) * out_rows + jnp.arange(out_rows, dtype=jnp.int32)
    part_ids = jnp.stack([col, col + 1 - 2 * place])[:, None] * part_local + jnp.arange(part_local, dtype=jnp.int32)
    keep = (hole_ids.reshape(-1, 1) < hh_used) & (part_ids.reshape(1, -1) < pp_used)
    both = jnp.concatenate([kept, taken], axis=1)
    both = jnp.where(keep, both, jnp.zeros_like(both))
    left = lax.all_gather(both, "row", axis=0, tiled=True)
    part = jnp.dot(left[:, :part_local], tile, preferred_element_type=jnp.float32)
    part = part + jnp.dot(left[:, part_local:], other_tile, preferred_element_type=jnp.float32)

    part = part.astype(jnp.bfloat16).reshape(NX, NZ // PAIR * out_rows, out_cols)
    got = lax.all_to_all(part, "x", 0, 0)
    some = add_up(got).astype(jnp.bfloat16)
    got = lax.all_to_all(some.reshape(NZ // PAIR, out_rows, out_cols), "zh", 0, 0)
    ladder = add_up(got)

    out_hole = col * out_rows + jnp.arange(out_rows, dtype=jnp.int32)
    out_part = y * out_cols + jnp.arange(out_cols, dtype=jnp.int32)
    row_ok, col_ok = out_hole < hh_used, out_part < pp_used
    hole, particle = hole_energy[0], part_energy[0][None, :]
    valid = row_ok[:, None] & col_ok[None, :]
    denom = hole[:, None] - particle
    value = (v_hhpp[0].astype(jnp.float32) + ladder) / denom
    result = jnp.where(valid, value, jnp.zeros_like(value)).astype(jnp.bfloat16)
    return result[None]


def solution(mesh):
    split = Mesh(mesh.devices.reshape(2, NY, NX, NZ // PAIR, PAIR), ("grp", "row", "x", "zh", "zl"))
    col = ("x", "zh", "zl")
    return jax.shard_map(
        local,
        mesh=split,
        in_specs=(
            P("grp", col, "row"),
            P("grp", "row", col),
            P("grp", col, "row"),
            P("grp", col),
            P("grp", "row"),
            P("grp"),
            P("grp"),
        ),
        out_specs=P("grp", col, "row"),
        check_vma=False,
    )
```

```python
import jax
import jax.numpy as jnp
from jax import lax
from jax.sharding import Mesh, PartitionSpec as P

NX, NZ, NY = 4, 8, 8
PAIR = 2


def add_up(parts):
    total = parts[0].astype(jnp.float32)
    for i in range(1, parts.shape[0]):
        total = total + parts[i].astype(jnp.float32)
    return total


def local(v_pppp, lam, v_hhpp, hole_energy, part_energy, pp_dim, hh_dim):
    pp_used = pp_dim[0]
    hh_used = hh_dim[0]
    hole_local = lam.shape[1]
    part_local = lam.shape[2]
    y = lax.axis_index("row")
    col = lax.axis_index(("x", "zh", "zl"))
    out_rows = v_hhpp.shape[1]
    out_cols = v_hhpp.shape[2]
    swap = [(0, 1), (1, 0)]

    halves = lam[0].reshape(hole_local // (PAIR * out_rows), PAIR, out_rows, part_local)
    half = (hole_local // PAIR, part_local)
    place = lax.axis_index("zl")
    given = lax.dynamic_slice_in_dim(halves, 1 - place, 1, 1).reshape(half)
    pair = lax.all_gather(given, "zl")
    tile, pair, halves = lax.optimization_barrier((v_pppp[0], pair, halves))
    kept = lax.dynamic_slice_in_dim(halves, place, 1, 1).reshape(half)
    taken = jnp.where(place == 1, pair[0], pair[1])
    other_tile = lax.ppermute(tile, "zl", swap)
    blocks = jnp.arange(hole_local // (PAIR * out_rows), dtype=jnp.int32)
    hole_ids = y * hole_local + (blocks[:, None] * PAIR + place) * out_rows + jnp.arange(out_rows, dtype=jnp.int32)
    part_ids = jnp.stack([col, col + 1 - 2 * place])[:, None] * part_local + jnp.arange(part_local, dtype=jnp.int32)
    keep = (hole_ids.reshape(-1, 1) < hh_used) & (part_ids.reshape(1, -1) < pp_used)
    both = jnp.concatenate([kept, taken], axis=1)
    both = jnp.where(keep, both, jnp.zeros_like(both))
    left = lax.all_gather(both, "row", axis=0, tiled=True)
    part = jnp.dot(left[:, :part_local], tile, preferred_element_type=jnp.float32)
    part = part + jnp.dot(left[:, part_local:], other_tile, preferred_element_type=jnp.float32)

    part = part.astype(jnp.bfloat16).reshape(NX, NZ // PAIR * out_rows, out_cols)
    got = lax.all_to_all(part, "x", 0, 0)
    some = add_up(got).astype(jnp.bfloat16)
    got = lax.all_to_all(some.reshape(NZ // PAIR, out_rows, out_cols), "zh", 0, 0)
    ladder = add_up(got)

    out_hole = col * out_rows + jnp.arange(out_rows, dtype=jnp.int32)
    out_part = y * out_cols + jnp.arange(out_cols, dtype=jnp.int32)
    row_ok, col_ok = out_hole < hh_used, out_part < pp_used
    hole, particle = hole_energy[0], part_energy[0][None, :]
    valid = row_ok[:, None] & col_ok[None, :]
    denom = hole[:, None] - particle
    value = (v_hhpp[0].astype(jnp.float32) + ladder) / denom
    result = jnp.where(valid, value, jnp.zeros_like(value)).astype(jnp.bfloat16)
    return result[None]


def solution(mesh):
    split = Mesh(mesh.devices.reshape(2, NY, NX, NZ // PAIR, PAIR), ("grp", "row", "x", "zh", "zl"))
    col = ("x", "zh", "zl")
    return jax.shard_map(
        local,
        mesh=split,
        in_specs=(
            P("grp", col, "row"),
            P("grp", "row", col),
            P("grp", col, "row"),
            P("grp", col),
            P("grp", "row"),
            P("grp"),
            P("grp"),
        ),
        out_specs=P("grp", col, "row"),
        check_vma=False,
    )
```

```python
import jax
import jax.numpy as jnp
from jax import lax
from jax.sharding import Mesh, PartitionSpec as P

NX, NZ, NY = 4, 8, 8
PAIR = 2


def add_up(parts):
    total = parts[0].astype(jnp.float32)
    for i in range(1, parts.shape[0]):
        total = total + parts[i].astype(jnp.float32)
    return total


def local(v_pppp, lam, v_hhpp, hole_energy, part_energy, pp_dim, hh_dim):
    pp_used = pp_dim[0]
    hh_used = hh_dim[0]
    hole_local = lam.shape[1]
    part_local = lam.shape[2]
    y = lax.axis_index("row")
    col = lax.axis_index(("x", "zh", "zl"))
    out_rows = v_hhpp.shape[1]
    out_cols = v_hhpp.shape[2]
    swap = [(0, 1), (1, 0)]

    halves = lam[0].reshape(hole_local // (PAIR * out_rows), PAIR, out_rows, part_local)
    half = (hole_local // PAIR, part_local)
    place = lax.axis_index("zl")
    kept = lax.dynamic_slice_in_dim(halves, place, 1, 1).reshape(half)
    given = lax.dynamic_slice_in_dim(halves, 1 - place, 1, 1).reshape(half)
    kept, given = lax.optimization_barrier((kept, given))
    pair = lax.all_gather(given, "zl")
    tile, pair = lax.optimization_barrier((v_pppp[0], pair))
    taken = jnp.where(place == 1, pair[0], pair[1])
    upper = lax.ppermute(tile[: part_local // 2], "zl", swap)
    lower = lax.ppermute(tile[part_local // 2 :], "zl", swap)
    blocks = jnp.arange(hole_local // (PAIR * out_rows), dtype=jnp.int32)
    hole_ids = y * hole_local + (blocks[:, None] * PAIR + place) * out_rows + jnp.arange(out_rows, dtype=jnp.int32)
    part_ids = jnp.stack([col, col + 1 - 2 * place])[:, None] * part_local + jnp.arange(part_local, dtype=jnp.int32)
    keep = (hole_ids.reshape(-1, 1) < hh_used) & (part_ids.reshape(1, -1) < pp_used)
    both = jnp.concatenate([kept, taken], axis=1)
    both = jnp.where(keep, both, jnp.zeros_like(both))
    left = lax.all_gather(both, "row", axis=0, tiled=True)
    part = jnp.dot(left[:, :part_local], tile, preferred_element_type=jnp.float32)
    part = part + jnp.dot(left[:, part_local:], jnp.concatenate([upper, lower], axis=0), preferred_element_type=jnp.float32)

    part = part.astype(jnp.bfloat16).reshape(NX, NZ // PAIR * out_rows, out_cols)
    got = lax.all_to_all(part, "x", 0, 0)
    some = add_up(got).astype(jnp.bfloat16)
    got = lax.all_to_all(some.reshape(NZ // PAIR, out_rows, out_cols), "zh", 0, 0)
    ladder = add_up(got)

    out_hole = col * out_rows + jnp.arange(out_rows, dtype=jnp.int32)
    out_part = y * out_cols + jnp.arange(out_cols, dtype=jnp.int32)
    row_ok, col_ok = out_hole < hh_used, out_part < pp_used
    hole, particle = hole_energy[0], part_energy[0][None, :]
    valid = row_ok[:, None] & col_ok[None, :]
    denom = hole[:, None] - particle
    value = (v_hhpp[0].astype(jnp.float32) + ladder) / denom
    result = jnp.where(valid, value, jnp.zeros_like(value)).astype(jnp.bfloat16)
    return result[None]


def solution(mesh):
    split = Mesh(mesh.devices.reshape(2, NY, NX, NZ // PAIR, PAIR), ("grp", "row", "x", "zh", "zl"))
    col = ("x", "zh", "zl")
    return jax.shard_map(
        local,
        mesh=split,
        in_specs=(
            P("grp", col, "row"),
            P("grp", "row", col),
            P("grp", col, "row"),
            P("grp", col),
            P("grp", "row"),
            P("grp"),
            P("grp"),
        ),
        out_specs=P("grp", col, "row"),
        check_vma=False,
    )
```
